32 devices in a mesh: blk: 4 (over x, core), grp: 8 (over z, y).
Axes of the slice: x: 2, y: 2, z: 4, core: 2. Of those that a mesh axis runs over, the one named last changes fastest.
Arguments:
- normals: bfloat16 [2048, 131072], P('blk', 'grp'), may hold values from -6 to 6
- mean_square: float32 [2048], P('blk'), may hold values from 0.5 to 2
- freedom_degrees: int32 [2048], P('blk'), may hold values from 3 to 30
- gamma_slab: bfloat16 [1024, 131072], P('blk', 'grp'), may hold values from -0.015625 to 0.015625
- deltas: bfloat16 [131072], P('grp'), may hold values from -0.5 to 0.5
- desk_map: int32 [131072], P('grp'), may hold values from 0 to 127
Outputs:
- desk_pnl: float32 [2048, 128], P(('blk', 'grp'))
The draws below stay inside these ranges and needn't reach their ends.
All inputs are finite; a program needn't handle non-finite values.
Results may differ from the reference program's by a relative error of at most 0.0038.
Values may be sent and summed in bfloat16 or wider, within the bound.
No kernel may reach another device: no remote copies, remote signals or barrier semaphores. Data moves between devices by JAX's collectives and lax.ppermute only.
A program may use at most 128 MiB of HBM per device.

```python
import math
import jax
import jax.numpy as jnp
from jax import lax

F = 131072
DESKS = 128
STRIDE = 128
SC_DEV = 512
R = 1024
S = 2048


def place_ends(entries, stream_key, smallest, largest):
    longest = entries.shape.index(max(entries.shape))
    spots = []
    for shift in (0, 1):
        where = [jax.random.randint(jax.random.fold_in(stream_key, axis), (), 0, length) for axis, length in enumerate(entries.shape)]
        where[longest] = (where[longest] + shift) % entries.shape[longest]
        spots.append(tuple(where))
    return entries.at[spots[0]].set(smallest).at[spots[1]].set(largest)


def block_levels(rng, dims, pieces, least, top_value):
    loudness, own = 1.0, jax.random.fold_in(rng, 6)
    for axis_at, parts in pieces:
        steps = jnp.exp(jax.random.uniform(jax.random.fold_in(own, axis_at), (parts,), jnp.float32, least / len(pieces), top_value / len(pieces)))
        loudness = loudness * jnp.repeat(steps, dims[axis_at] // parts).reshape([-1 if axis == axis_at else 1 for axis in range(len(dims))])
    return loudness


def bell_draw(rng, shape, deviation, most, split=(), held_as=jnp.bfloat16):
    array = jax.random.normal(rng, shape, jnp.float32) * deviation
    if len(split) > 0:
        array = block_levels(rng, shape, split, -0.22, 0.18) * array
    return jnp.clip(array, min=-most, max=most).astype(held_as)


def setup_inputs(seed: int = 0) -> dict:
    key_of = jax.random.split(jax.random.key(seed), 7)
    return {
        "normals": bell_draw(key_of[0], (S, F), 1.0, 6.0, ((0, 4), (1, 8))),
        "mean_square": jnp.clip(jnp.exp(math.log(2.0) - 1.3862944 * jax.random.uniform(key_of[1], (S,), jnp.float32) ** block_levels(key_of[1], (S,), ((0, 4),), -0.2, 0.2)), 0.5, 2.0),
        "freedom_degrees": place_ends(jax.random.randint(key_of[2], (S,), 3, 31), jax.random.fold_in(key_of[2], 1), 3, 30).astype(jnp.int32),
        "gamma_slab": bell_draw(key_of[3], (R, F), F ** -0.5, 0.015625, ((0, 4), (1, 8))),
        "deltas": bell_draw(key_of[4], (F,), ((DESKS / F) ** 0.5), 0.5, ((0, 8),)),
        "desk_map": place_ends(jax.random.randint(key_of[5], (F,), 0, DESKS), jax.random.fold_in(key_of[5], 1), 0, DESKS - 1).astype(jnp.int32),
    }


def reference(normals, mean_square, freedom_degrees, gamma_slab, deltas, desk_map):
    degrees = freedom_degrees.astype(jnp.float32)
    scaling = jnp.sqrt((degrees - 2.0) / degrees / mean_square)
    levels = jnp.arange(DESKS, dtype=jnp.int32)
    weights = jnp.where(desk_map[:, None] == levels[None, :], deltas[:, None], jnp.zeros((), deltas.dtype)).astype(jnp.bfloat16)
    window_hot = (desk_map[::STRIDE][:, None] == levels[None, :]).astype(jnp.float32)
    block_rows = SC_DEV

    def one_block(index):
        first = (index * block_rows).astype(jnp.int32)
        draws = lax.dynamic_slice_in_dim(normals, first, block_rows, 0)
        factors = lax.dynamic_slice_in_dim(scaling, first, block_rows, 0)
        shocks = (draws.astype(jnp.float32) * factors[:, None]).astype(jnp.bfloat16)
        moved = jnp.dot(shocks, gamma_slab.T, preferred_element_type=jnp.float32)
        quadratic = shocks[:, ::STRIDE].astype(jnp.float32) * moved
        linear = jnp.dot(shocks, weights, preferred_element_type=jnp.float32)
        return linear + 0.5 * jnp.dot(quadratic, window_hot, precision=lax.Precision.HIGHEST, preferred_element_type=jnp.float32)
    blocks = lax.map(one_block, jnp.arange(normals.shape[0] // block_rows, dtype=jnp.int32))
    return blocks.reshape(normals.shape[0], DESKS)
```

```python
import functools

import jax
import jax.numpy as jnp
from jax import lax
from jax.experimental import pallas as pl
from jax.experimental.pallas import tpu as pltpu
from jax.sharding import PartitionSpec as P

DESKS = 128
STRIDE = 128
CORES = 2
PARTS = (1, 15, 10, 4, 1, 1)
EARLY = 3
VMEM_BYTES = 40 * 2**20

F32 = jnp.float32
BF16 = jnp.bfloat16


def dot_t(left, right):
    return lax.dot_general(left, right, (((1,), (1,)), ((), ())), preferred_element_type=F32)


def call(kernel, **options):
    return pl.pallas_call(
        kernel, compiler_params=pltpu.CompilerParams(vmem_limit_bytes=VMEM_BYTES), **options
    )


def whole(shape):
    return pl.BlockSpec(shape, lambda *_: (0,) * len(shape))


def shock_kernel(blocks, grp_ref, normals_ref, scaling_ref, desks_ref, deltas_ref, shocks_ref, sums_ref):
    step = pl.program_id(0)
    height = normals_ref.shape[0] // blocks
    width = normals_ref.shape[1]
    for index in range(blocks):
        source = pl.ds(pl.multiple_of((index ^ grp_ref[0]) * height, height), height)
        scaled = normals_ref[source, :].astype(F32) * scaling_ref[source, :]
        shocks_ref[index * height : (index + 1) * height, :] = scaled.astype(BF16)
    level = lax.broadcasted_iota(jnp.int32, (DESKS, width), 0)
    factor = lax.broadcasted_iota(jnp.int32, (STRIDE, width), 1) + step * width
    entry = lax.broadcasted_iota(jnp.int32, (STRIDE, width), 0)
    weights = jnp.where(level == desks_ref[...], deltas_ref[...], 0.0).astype(BF16)
    chosen = jnp.where(factor == entry * STRIDE, 1.0, 0.0).astype(BF16)
    sums = dot_t(shocks_ref[...], jnp.concatenate([weights, chosen], 0))

    @pl.when(step == 0)
    def _():
        sums_ref[...] = sums

    @pl.when(step > 0)
    def _():
        sums_ref[...] += sums


def make_shocks(normals, scaling, grp, blocks, desks, deltas):
    rows, cols = normals.shape
    width = min(cols, 2048)
    tile = pl.BlockSpec((rows, width), lambda j, _: (0, j))
    vector = pl.BlockSpec((1, width), lambda j, _: (0, j))
    return call(
        functools.partial(shock_kernel, blocks),
        grid_spec=pltpu.PrefetchScalarGridSpec(
            num_scalar_prefetch=1,
            grid=(cols // width,),
            in_specs=[tile, whole((rows, 1)), vector, vector],
            out_specs=[tile, whole((rows, DESKS + STRIDE))],
        ),
        out_shape=[
            jax.ShapeDtypeStruct((rows, cols), BF16),
            jax.ShapeDtypeStruct((rows, DESKS + STRIDE), F32),
        ],
        name="shocks",
    )(grp[None], normals, scaling[:, None], desks[None, :], deltas.astype(F32)[None, :])


def moved_kernel(has_start, *refs):
    own_ref, sibling_ref, gamma_ref, *start_ref, out_ref = refs
    half = own_ref.shape[0]

    @pl.when(pl.program_id(0) == 0)
    def _():
        out_ref[...] = start_ref[0][...] if has_start else jnp.zeros_like(out_ref)

    gamma = gamma_ref[...]
    out_ref[:half] += dot_t(own_ref[...], gamma)
    out_ref[half:] += dot_t(sibling_ref[...], gamma)


def add_moved(own, sibling, gamma, first, start=None):
    rows, (count, cols) = own.shape[0], gamma.shape
    width = next(size for size in (1024, 512, 256, 128) if cols % size == 0 and first % size == 0)
    shocks = pl.BlockSpec((rows, width), lambda j: (0, j + first // width))
    return call(
        functools.partial(moved_kernel, start is not None),
        grid=(cols // width,),
        in_specs=[shocks, shocks, pl.BlockSpec((count, width), lambda j: (0, j))]
        + [whole((2 * rows, count))] * (start is not None),
        out_specs=whole((2 * rows, count)),
        out_shape=jax.ShapeDtypeStruct((2 * rows, count), F32),
        name="moved",
    )(own, sibling, gamma, *([] if start is None else [start]))


def by_desk(moved, window, hot):
    quadratic = 0.5 * window.astype(F32) * moved
    total = None
    for _ in range(3):
        piece = quadratic.astype(BF16)
        quadratic = quadratic - piece.astype(F32)
        product = jnp.dot(piece, hot, preferred_element_type=F32)
        total = product if total is None else total + product
    return total


def early_kernel(linear_ref, *refs):
    *groups, mine_ref, theirs_ref = refs
    half = mine_ref.shape[0]
    total = None
    for index in range(0, len(groups), 3):
        moved_ref, window_ref, hot_ref = groups[index : index + 3]
        terms = by_desk(moved_ref[...], window_ref[...], hot_ref[...])
        total = terms if total is None else total + terms
    mine_ref[...] = total[:half] + linear_ref[...]
    theirs_ref[...] = total[half:]


def early_terms(linear, *groups):
    shape = jax.ShapeDtypeStruct(linear.shape, F32)
    return call(early_kernel, out_shape=[shape, shape], name="early")(linear, *groups)


def late_kernel(own_ref, sibling_ref, gamma_ref, start_ref, window_ref, hot_ref, mine_ref, theirs_ref):
    gamma, hot, half = gamma_ref[...], hot_ref[...], own_ref.shape[0]
    moved = start_ref[half:] + dot_t(sibling_ref[...], gamma)
    theirs_ref[...] = by_desk(moved, window_ref[half:], hot).astype(BF16)
    moved = start_ref[:half] + dot_t(own_ref[...], gamma)
    mine_ref[...] = by_desk(moved, window_ref[:half], hot)


def late_terms(own, sibling, gamma, first, start, window, hot):
    rows, (count, cols) = own.shape[0], gamma.shape
    shocks = pl.BlockSpec((rows, cols), lambda _: (0, first // cols))
    return call(
        late_kernel,
        grid=(1,),
        in_specs=[shocks, shocks]
        + [whole(shape) for shape in (gamma.shape, start.shape, window.shape, hot.shape)],
        out_specs=[whole((rows, DESKS)), whole((rows, DESKS))],
        out_shape=[jax.ShapeDtypeStruct((rows, DESKS), F32), jax.ShapeDtypeStruct((rows, DESKS), BF16)],
        name="late",
    )(own, sibling, gamma, start, window, hot)


def local(n_blk, n_grp, normals, mean_square, freedom_degrees, gamma_slab, deltas, desk_map):
    together = lax.optimization_barrier
    blk, grp = lax.axis_index("blk"), lax.axis_index("grp")
    scenarios, columns = normals.shape
    rows = gamma_slab.shape[0]
    chips = n_blk // CORES
    block = scenarios // n_grp
    per_grp = columns // STRIDE
    sibling = [(i, i ^ 1) for i in range(n_blk)]

    def to_sibling(array):
        return lax.ppermute(array, "blk", sibling)

    def from_chips(array):
        parts = [
            lax.ppermute(array, "blk", [(i, (i + CORES * step) % n_blk) for i in range(n_blk)])
            for step in range(1, chips)
        ]
        return parts[0] if len(parts) == 1 else jnp.concatenate(parts, 0)

    def window_of(array, axis):
        own = lax.dynamic_slice_in_dim(array, blk * rows, rows, axis)
        others = [
            lax.dynamic_slice_in_dim(array, lax.rem(blk + n_blk - CORES * step, n_blk) * rows, rows, axis)
            for step in range(1, chips)
        ]
        return own, others[0] if len(others) == 1 else jnp.concatenate(others, axis)

    unit = columns // sum(PARTS)
    starts = [sum(PARTS[:i]) * unit for i in range(len(PARTS) + 1)]
    last = len(PARTS) - 1

    def chunk(index):
        return gamma_slab[:, starts[index] : starts[index + 1]]

    first = chunk(0)
    first, gamma_slab = together((first, gamma_slab))
    arrived = [from_chips(first)] + [from_chips(chunk(index)) for index in range(1, len(PARTS))]
    normals, arrived[0] = together((normals, arrived[0]))

    degrees = freedom_degrees.astype(F32)
    scaling = jnp.sqrt((degrees - 2.0) / degrees / mean_square)
    own, sums = make_shocks(normals, scaling, grp, n_grp, desk_map, deltas)
    other = to_sibling(own)
    linear = sums[:, :DESKS]

    order = jnp.arange(n_grp, dtype=jnp.int32) ^ grp
    plain = jnp.take(sums[:, DESKS : DESKS + per_grp].reshape(n_grp, block, per_grp), order, axis=0)
    window_desks = jnp.broadcast_to(desk_map[::STRIDE].astype(F32), (16, per_grp))
    packed = jnp.concatenate([plain.reshape(scenarios, per_grp), window_desks], 0).astype(BF16)
    packed = lax.all_to_all(jnp.broadcast_to(packed, (n_grp,) + packed.shape), "grp", 0, 0, tiled=True)
    desks = packed[:, scenarios].reshape(-1)
    hot = (desks[:, None] == jnp.arange(DESKS).astype(BF16)[None, :]).astype(BF16)
    own_hot, other_hot = window_of(hot, 0)
    window = packed[:, :scenarios].reshape(n_grp, n_grp, block, per_grp)
    window = jnp.take(window, order, axis=1).transpose(1, 2, 0, 3).reshape(scenarios, n_grp * per_grp)
    window = jnp.concatenate([window, to_sibling(window)], 0)
    own_window, other_window = window_of(window, 1)

    own_moved = add_moved(own, other, gamma_slab, 0)
    moved = None
    for index in range(EARLY):
        moved = add_moved(own, other, arrived[index], starts[index], moved)
    mine, theirs = early_terms(linear, own_moved, own_window, own_hot, moved, other_window, other_hot)
    mine = jnp.take((mine + to_sibling(theirs)).reshape(n_grp, block, DESKS), order, axis=0)
    early = lax.all_to_all(mine, "grp", 0, 0, tiled=True).sum(0)

    moved = None
    for index in range(EARLY, last):
        moved = add_moved(own, other, arrived[index], starts[index], moved)
    final, early = together((arrived[last], early))
    mine, theirs = late_terms(own, other, final, starts[last], moved, other_window, other_hot)
    late = mine + to_sibling(theirs).astype(F32)
    late = late.reshape(n_grp, block, DESKS)
    bit = 1
    while bit < n_grp:
        halves = late.reshape(late.shape[0] // 2, 2, block, DESKS)
        sent = lax.ppermute(halves[:, 1].astype(BF16), "grp", [(i, i ^ bit) for i in range(n_grp)])
        late = halves[:, 0] + sent.astype(F32)
        bit *= 2
    return early + late[0]


def solution(mesh):
    in_specs = (P("blk", "grp"), P("blk"), P("blk"), P("blk", "grp"), P("grp"), P("grp"))
    out_specs = P(("blk", "grp"), None)
    body = functools.partial(local, mesh.shape["blk"], mesh.shape["grp"])
    return jax.shard_map(body, mesh=mesh, in_specs=in_specs, out_specs=out_specs, check_vma=False)
```

```python
import functools

import jax
import jax.numpy as jnp
from jax import lax
from jax.experimental import pallas as pl
from jax.experimental.pallas import tpu as pltpu
from jax.sharding import PartitionSpec as P

DESKS = 128
STRIDE = 128
CORES = 2
PARTS = (5, 15, 9, 2, 1)
EARLY = 2
VMEM_BYTES = 40 * 2**20

F32 = jnp.float32
BF16 = jnp.bfloat16


def dot_t(left, right):
    return lax.dot_general(left, right, (((1,), (1,)), ((), ())), preferred_element_type=F32)


def call(kernel, **options):
    return pl.pallas_call(
        kernel, compiler_params=pltpu.CompilerParams(vmem_limit_bytes=VMEM_BYTES), **options
    )


def whole(shape):
    return pl.BlockSpec(shape, lambda *_: (0,) * len(shape))


def scaled(normals_ref, scaling_ref):
    return (normals_ref[...].astype(F32) * scaling_ref[...]).astype(BF16)


def own_kernel(own_ref, sibling_ref, own_scaling_ref, sibling_scaling_ref, gamma_ref, desks_ref, deltas_ref, moved_ref, sums_ref):
    step = pl.program_id(0)
    half, width = own_ref.shape

    @pl.when(step == 0)
    def _():
        moved_ref[...] = jnp.zeros_like(moved_ref)
        sums_ref[...] = jnp.zeros_like(sums_ref)

    level = lax.broadcasted_iota(jnp.int32, (DESKS, width), 0)
    factor = lax.broadcasted_iota(jnp.int32, (STRIDE, width), 1) + step * width
    entry = lax.broadcasted_iota(jnp.int32, (STRIDE, width), 0)
    weights = jnp.where(level == desks_ref[...], deltas_ref[...], 0.0).astype(BF16)
    chosen = jnp.where(factor == entry * STRIDE, 1.0, 0.0).astype(BF16)
    own, gamma = scaled(own_ref, own_scaling_ref), gamma_ref[...]
    sums_ref[...] += dot_t(own, jnp.concatenate([weights, chosen], 0))
    moved_ref[:half] += dot_t(own, gamma)
    moved_ref[half:] += dot_t(scaled(sibling_ref, sibling_scaling_ref), gamma)


def own_moved(own, sibling, own_scaling, sibling_scaling, gamma, desks, deltas):
    rows, (count, cols) = own.shape[0], gamma.shape
    width = min(cols, 1024)
    normals = pl.BlockSpec((rows, width), lambda j: (0, j))
    vector = pl.BlockSpec((1, width), lambda j: (0, j))
    return call(
        own_kernel,
        grid=(cols // width,),
        in_specs=[normals, normals, whole((rows, 1)), whole((rows, 1))]
        + [pl.BlockSpec((count, width), lambda j: (0, j)), vector, vector],
        out_specs=[whole((2 * rows, count)), whole((rows, DESKS + STRIDE))],
        out_shape=[
            jax.ShapeDtypeStruct((2 * rows, count), F32),
            jax.ShapeDtypeStruct((rows, DESKS + STRIDE), F32),
        ],
        name="own_rows",
    )(own, sibling, own_scaling, sibling_scaling, gamma, desks[None, :], deltas.astype(F32)[None, :])


def moved_kernel(has_start, *refs):
    own_ref, sibling_ref, own_scaling_ref, sibling_scaling_ref, gamma_ref, *start_ref, out_ref = refs
    half = own_ref.shape[0]

    @pl.when(pl.program_id(0) == 0)
    def _():
        out_ref[...] = start_ref[0][...] if has_start else jnp.zeros_like(out_ref)

    gamma = gamma_ref[...]
    out_ref[:half] += dot_t(scaled(own_ref, own_scaling_ref), gamma)
    out_ref[half:] += dot_t(scaled(sibling_ref, sibling_scaling_ref), gamma)


def add_moved(own, sibling, own_scaling, sibling_scaling, gamma, first, start=None):
    rows, (count, cols) = own.shape[0], gamma.shape
    width = next(size for size in (1024, 512, 256, 128) if cols % size == 0 and first % size == 0)
    normals = pl.BlockSpec((rows, width), lambda j: (0, j + first // width))
    return call(
        functools.partial(moved_kernel, start is not None),
        grid=(cols // width,),
        in_specs=[normals, normals, whole((rows, 1)), whole((rows, 1))]
        + [pl.BlockSpec((count, width), lambda j: (0, j))]
        + [whole((2 * rows, count))] * (start is not None),
        out_specs=whole((2 * rows, count)),
        out_shape=jax.ShapeDtypeStruct((2 * rows, count), F32),
        name="moved",
    )(own, sibling, own_scaling, sibling_scaling, gamma, *([] if start is None else [start]))


def by_desk(moved, window, hot):
    quadratic = 0.5 * window.astype(F32) * moved
    total = None
    for _ in range(3):
        piece = quadratic.astype(BF16)
        quadratic = quadratic - piece.astype(F32)
        product = jnp.dot(piece, hot, preferred_element_type=F32)
        total = product if total is None else total + product
    return total


def early_kernel(linear_ref, *refs):
    *groups, mine_ref, theirs_ref = refs
    half = mine_ref.shape[0]
    total = None
    for index in range(0, len(groups), 3):
        moved_ref, window_ref, hot_ref = groups[index : index + 3]
        terms = by_desk(moved_ref[...], window_ref[...], hot_ref[...])
        total = terms if total is None else total + terms
    mine_ref[...] = total[:half] + linear_ref[...]
    theirs_ref[...] = total[half:]


def early_terms(linear, *groups):
    shape = jax.ShapeDtypeStruct(linear.shape, F32)
    return call(early_kernel, out_shape=[shape, shape], name="early")(linear, *groups)


def late_kernel(
    blocks,
    grp_ref,
    own_ref,
    sibling_ref,
    own_scaling_ref,
    sibling_scaling_ref,
    gamma_ref,
    start_ref,
    window_ref,
    hot_ref,
    mine_ref,
    theirs_ref,
    terms_ref,
):
    gamma, hot, half = gamma_ref[...], hot_ref[...], own_ref.shape[0]
    moved = start_ref[half:] + dot_t(scaled(sibling_ref, sibling_scaling_ref), gamma)
    terms_ref[half:] = by_desk(moved, window_ref[half:], hot)
    moved = start_ref[:half] + dot_t(scaled(own_ref, own_scaling_ref), gamma)
    terms_ref[:half] = by_desk(moved, window_ref[:half], hot)
    height = half // blocks
    for index in range(blocks):
        source = pl.multiple_of((index ^ grp_ref[0]) * height, height)
        place = slice(index * height, (index + 1) * height)
        mine_ref[place, :] = terms_ref[pl.ds(source, height), :]
        theirs_ref[place, :] = terms_ref[pl.ds(half + source, height), :].astype(BF16)


def late_terms(grp, blocks, own, sibling, own_scaling, sibling_scaling, gamma, first, start, window, hot):
    rows, (count, cols) = own.shape[0], gamma.shape
    normals = pl.BlockSpec((rows, cols), lambda *_: (0, first // cols))
    return call(
        functools.partial(late_kernel, blocks),
        grid_spec=pltpu.PrefetchScalarGridSpec(
            num_scalar_prefetch=1,
            grid=(1,),
            in_specs=[normals, normals, whole((rows, 1)), whole((rows, 1))]
            + [whole(shape) for shape in (gamma.shape, start.shape, window.shape, hot.shape)],
            out_specs=[whole((rows, DESKS)), whole((rows, DESKS))],
            scratch_shapes=[pltpu.VMEM((2 * rows, DESKS), F32)],
        ),
        out_shape=[jax.ShapeDtypeStruct((rows, DESKS), F32), jax.ShapeDtypeStruct((rows, DESKS), BF16)],
        name="late",
    )(grp[None], own, sibling, own_scaling, sibling_scaling, gamma, start, window, hot)


def local(n_blk, n_grp, normals, mean_square, freedom_degrees, gamma_slab, deltas, desk_map):
    together = lax.optimization_barrier
    blk, grp = lax.axis_index("blk"), lax.axis_index("grp")
    scenarios, columns = normals.shape
    rows = gamma_slab.shape[0]
    chips = n_blk // CORES
    block = scenarios // n_grp
    per_grp = columns // STRIDE
    sibling = [(i, i ^ 1) for i in range(n_blk)]

    def to_sibling(array):
        return lax.ppermute(array, "blk", sibling)

    def from_chips(array):
        parts = [
            lax.ppermute(array, "blk", [(i, (i + CORES * step) % n_blk) for i in range(n_blk)])
            for step in range(1, chips)
        ]
        return parts[0] if len(parts) == 1 else jnp.concatenate(parts, 0)

    def window_of(array, axis):
        own = lax.dynamic_slice_in_dim(array, blk * rows, rows, axis)
        others = [
            lax.dynamic_slice_in_dim(array, lax.rem(blk + n_blk - CORES * step, n_blk) * rows, rows, axis)
            for step in range(1, chips)
        ]
        return own, others[0] if len(others) == 1 else jnp.concatenate(others, axis)

    unit = columns // sum(PARTS)
    starts = [sum(PARTS[:i]) * unit for i in range(len(PARTS) + 1)]
    last = len(PARTS) - 1

    def chunk(index):
        return gamma_slab[:, starts[index] : starts[index + 1]]

    other = to_sibling(normals)
    first = chunk(0)
    first, gamma_slab = together((first, gamma_slab))
    arrived = [from_chips(first)] + [from_chips(chunk(index)) for index in range(1, len(PARTS))]
    gamma_slab, arrived[0] = together((gamma_slab, arrived[0]))

    degrees = freedom_degrees.astype(F32)
    scaling = jnp.sqrt((degrees - 2.0) / degrees / mean_square)[:, None]
    sides = (normals, other, scaling, to_sibling(scaling))
    own_rows, sums = own_moved(*sides, gamma_slab, desk_map, deltas)
    linear = sums[:, :DESKS]

    window_desks = jnp.broadcast_to(desk_map[::STRIDE].astype(F32), (16, per_grp))
    packed = jnp.concatenate([sums[:, DESKS : DESKS + per_grp], window_desks], 0).astype(BF16)
    packed = lax.all_to_all(jnp.broadcast_to(packed, (n_grp,) + packed.shape), "grp", 0, 0, tiled=True)
    desks = packed[:, scenarios].reshape(-1)
    hot = (desks[:, None] == jnp.arange(DESKS).astype(BF16)[None, :]).astype(BF16)
    own_hot, other_hot = window_of(hot, 0)
    window = packed[:, :scenarios].transpose(1, 0, 2).reshape(scenarios, n_grp * per_grp)
    window = jnp.concatenate([window, to_sibling(window)], 0)
    own_window, other_window = window_of(window, 1)

    moved = None
    for index in range(EARLY):
        moved = add_moved(*sides, arrived[index], starts[index], moved)
    mine, theirs = early_terms(linear, own_rows, own_window, own_hot, moved, other_window, other_hot)
    mine = (mine + to_sibling(theirs)).reshape(n_grp, block, DESKS)
    early = lax.all_to_all(mine, "grp", 0, 0, tiled=True).sum(0)

    moved = None
    for index in range(EARLY, last):
        moved = add_moved(*sides, arrived[index], starts[index], moved)
    final, early = together((arrived[last], early))
    mine, theirs = late_terms(grp, n_grp, *sides, final, starts[last], moved, other_window, other_hot)
    late = mine + to_sibling(theirs).astype(F32)
    late = late.reshape(n_grp, block, DESKS)
    bit = 1
    while bit < n_grp:
        halves = late.reshape(late.shape[0] // 2, 2, block, DESKS)
        sent = lax.ppermute(halves[:, 1].astype(BF16), "grp", [(i, i ^ bit) for i in range(n_grp)])
        late = halves[:, 0] + sent.astype(F32)
        bit *= 2
    return early + late[0]


def solution(mesh):
    in_specs = (P("blk", "grp"), P("blk"), P("blk"), P("blk", "grp"), P("grp"), P("grp"))
    out_specs = P(("blk", "grp"), None)
    body = functools.partial(local, mesh.shape["blk"], mesh.shape["grp"])
    return jax.shard_map(body, mesh=mesh, in_specs=in_specs, out_specs=out_specs, check_vma=False)
```

```python
import functools

import jax
import jax.numpy as jnp
from jax import lax
from jax.experimental import pallas as pl
from jax.experimental.pallas import tpu as pltpu
from jax.sharding import PartitionSpec as P

DESKS = 128
STRIDE = 128
CORES = 2
PARTS = (5, 15, 8, 3, 1)
EARLY = 2
VMEM_BYTES = 40 * 2**20

F32 = jnp.float32
BF16 = jnp.bfloat16


def dot_t(left, right):
    return lax.dot_general(left, right, (((1,), (1,)), ((), ())), preferred_element_type=F32)


def call(kernel, **options):
    return pl.pallas_call(
        kernel, compiler_params=pltpu.CompilerParams(vmem_limit_bytes=VMEM_BYTES), **options
    )


def whole(shape):
    return pl.BlockSpec(shape, lambda *_: (0,) * len(shape))


def scaled(normals_ref, scaling_ref):
    return (normals_ref[...].astype(F32) * scaling_ref[...]).astype(BF16)


def own_kernel(own_ref, sibling_ref, own_scaling_ref, sibling_scaling_ref, gamma_ref, desks_ref, deltas_ref, moved_ref, sums_ref):
    step = pl.program_id(0)
    half, width = own_ref.shape

    @pl.when(step == 0)
    def _():
        moved_ref[...] = jnp.zeros_like(moved_ref)
        sums_ref[...] = jnp.zeros_like(sums_ref)

    level = lax.broadcasted_iota(jnp.int32, (DESKS, width), 0)
    factor = lax.broadcasted_iota(jnp.int32, (STRIDE, width), 1) + step * width
    entry = lax.broadcasted_iota(jnp.int32, (STRIDE, width), 0)
    weights = jnp.where(level == desks_ref[...], deltas_ref[...], 0.0).astype(BF16)
    chosen = jnp.where(factor == entry * STRIDE, 1.0, 0.0).astype(BF16)
    own, gamma = scaled(own_ref, own_scaling_ref), gamma_ref[...]
    sums_ref[...] += dot_t(own, jnp.concatenate([weights, chosen], 0))
    moved_ref[:half] += dot_t(own, gamma)
    moved_ref[half:] += dot_t(scaled(sibling_ref, sibling_scaling_ref), gamma)


def own_moved(own, sibling, own_scaling, sibling_scaling, gamma, desks, deltas):
    rows, (count, cols) = own.shape[0], gamma.shape
    width = min(cols, 1024)
    normals = pl.BlockSpec((rows, width), lambda j: (0, j))
    vector = pl.BlockSpec((1, width), lambda j: (0, j))
    return call(
        own_kernel,
        grid=(cols // width,),
        in_specs=[normals, normals, whole((rows, 1)), whole((rows, 1))]
        + [pl.BlockSpec((count, width), lambda j: (0, j)), vector, vector],
        out_specs=[whole((2 * rows, count)), whole((rows, DESKS + STRIDE))],
        out_shape=[
            jax.ShapeDtypeStruct((2 * rows, count), F32),
            jax.ShapeDtypeStruct((rows, DESKS + STRIDE), F32),
        ],
        name="own_rows",
    )(own, sibling, own_scaling, sibling_scaling, gamma, desks[None, :], deltas.astype(F32)[None, :])


def moved_kernel(has_start, *refs):
    own_ref, sibling_ref, own_scaling_ref, sibling_scaling_ref, gamma_ref, *start_ref, out_ref = refs
    half = own_ref.shape[0]

    @pl.when(pl.program_id(0) == 0)
    def _():
        out_ref[...] = start_ref[0][...] if has_start else jnp.zeros_like(out_ref)

    gamma = gamma_ref[...]
    out_ref[:half] += dot_t(scaled(own_ref, own_scaling_ref), gamma)
    out_ref[half:] += dot_t(scaled(sibling_ref, sibling_scaling_ref), gamma)


def add_moved(own, sibling, own_scaling, sibling_scaling, gamma, first, start=None):
    rows, (count, cols) = own.shape[0], gamma.shape
    width = next(size for size in (1024, 512, 256, 128) if cols % size == 0 and first % size == 0)
    normals = pl.BlockSpec((rows, width), lambda j: (0, j + first // width))
    return call(
        functools.partial(moved_kernel, start is not None),
        grid=(cols // width,),
        in_specs=[normals, normals, whole((rows, 1)), whole((rows, 1))]
        + [pl.BlockSpec((count, width), lambda j: (0, j))]
        + [whole((2 * rows, count))] * (start is not None),
        out_specs=whole((2 * rows, count)),
        out_shape=jax.ShapeDtypeStruct((2 * rows, count), F32),
        name="moved",
    )(own, sibling, own_scaling, sibling_scaling, gamma, *([] if start is None else [start]))


def by_desk(moved, window, hot, pieces=3):
    quadratic = 0.5 * window.astype(F32) * moved
    total = None
    for _ in range(pieces):
        piece = quadratic.astype(BF16)
        quadratic = quadratic - piece.astype(F32)
        product = jnp.dot(piece, hot, preferred_element_type=F32)
        total = product if total is None else total + product
    return total


def early_kernel(linear_ref, *refs):
    *groups, mine_ref, theirs_ref = refs
    half = mine_ref.shape[0]
    total = None
    for index in range(0, len(groups), 3):
        moved_ref, window_ref, hot_ref = groups[index : index + 3]
        terms = by_desk(moved_ref[...], window_ref[...], hot_ref[...])
        total = terms if total is None else total + terms
    mine_ref[...] = total[:half] + linear_ref[...]
    theirs_ref[...] = total[half:]


def early_terms(linear, *groups):
    shape = jax.ShapeDtypeStruct(linear.shape, F32)
    return call(early_kernel, out_shape=[shape, shape], name="early")(linear, *groups)


def middle_kernel(own_ref, sibling_ref, own_scaling_ref, sibling_scaling_ref, gamma_ref, start_ref, window_ref, hot_ref, terms_ref, moved_ref):
    step = pl.program_id(0)
    half = own_ref.shape[0]

    @pl.when(step == 0)
    def _():
        moved_ref[...] = start_ref[...]

    gamma = gamma_ref[...]
    moved_ref[:half] += dot_t(scaled(own_ref, own_scaling_ref), gamma)
    moved_ref[half:] += dot_t(scaled(sibling_ref, sibling_scaling_ref), gamma)

    @pl.when(step == pl.num_programs(0) - 1)
    def _():
        terms_ref[...] = by_desk(moved_ref[...], window_ref[...], hot_ref[...], 2)


def middle_terms(own, sibling, own_scaling, sibling_scaling, gamma, first, start, window, hot):
    rows, (count, cols) = own.shape[0], gamma.shape
    width = next(size for size in (256, 128) if cols % size == 0 and first % size == 0)
    normals = pl.BlockSpec((rows, width), lambda j: (0, j + first // width))
    return call(
        middle_kernel,
        grid=(cols // width,),
        in_specs=[normals, normals, whole((rows, 1)), whole((rows, 1))]
        + [pl.BlockSpec((count, width), lambda j: (0, j))]
        + [whole(shape) for shape in (start.shape, window.shape, hot.shape)],
        out_specs=whole((2 * rows, DESKS)),
        out_shape=jax.ShapeDtypeStruct((2 * rows, DESKS), F32),
        scratch_shapes=[pltpu.VMEM((2 * rows, count), F32)],
        name="middle",
    )(own, sibling, own_scaling, sibling_scaling, gamma, start, window, hot)


def late_kernel(blocks, first, grp_ref, normals_ref, scaling_ref, gamma_ref, start_ref, window_ref, hot_ref, out_ref, terms_ref):
    half = normals_ref.shape[0]
    place = slice(first, first + half)
    moved = dot_t(scaled(normals_ref, scaling_ref), gamma_ref[...])
    terms_ref[...] = start_ref[place] + by_desk(moved, window_ref[place], hot_ref[...], 1)
    height = half // blocks
    for index in range(blocks):
        source = pl.multiple_of((index ^ grp_ref[0]) * height, height)
        out_ref[index * height : (index + 1) * height, :] = terms_ref[pl.ds(source, height), :].astype(out_ref.dtype)


def late_terms(grp, blocks, side, kind, normals, scaling, gamma, start, window, hot):
    rows = normals.shape[0]
    in_vmem = pl.BlockSpec(memory_space=pltpu.VMEM)
    return pl.pallas_call(
        functools.partial(late_kernel, blocks, side * rows),
        in_specs=[pl.BlockSpec(memory_space=pltpu.SMEM)] + [in_vmem] * 6,
        out_specs=in_vmem,
        scratch_shapes=[pltpu.VMEM((rows, DESKS), F32)],
        out_shape=jax.ShapeDtypeStruct((rows, DESKS), kind),
        compiler_params=pltpu.CompilerParams(vmem_limit_bytes=12 * 2**20),
        name="late",
    )(grp[None], normals, scaling, gamma, start, window, hot)


def local(n_blk, n_grp, normals, mean_square, freedom_degrees, gamma_slab, deltas, desk_map):
    together = lax.optimization_barrier
    blk, grp = lax.axis_index("blk"), lax.axis_index("grp")
    scenarios, columns = normals.shape
    rows = gamma_slab.shape[0]
    chips = n_blk // CORES
    block = scenarios // n_grp
    per_grp = columns // STRIDE
    sibling = [(i, i ^ 1) for i in range(n_blk)]

    def to_sibling(array):
        return lax.ppermute(array, "blk", sibling)

    def from_chips(array):
        parts = [
            lax.ppermute(array, "blk", [(i, (i + CORES * step) % n_blk) for i in range(n_blk)])
            for step in range(1, chips)
        ]
        return parts[0] if len(parts) == 1 else jnp.concatenate(parts, 0)

    def window_of(array, axis):
        own = lax.dynamic_slice_in_dim(array, blk * rows, rows, axis)
        others = [
            lax.dynamic_slice_in_dim(array, lax.rem(blk + n_blk - CORES * step, n_blk) * rows, rows, axis)
            for step in range(1, chips)
        ]
        return own, others[0] if len(others) == 1 else jnp.concatenate(others, axis)

    unit = columns // sum(PARTS)
    starts = [sum(PARTS[:i]) * unit for i in range(len(PARTS) + 1)]
    last = len(PARTS) - 1

    def chunk(index):
        return gamma_slab[:, starts[index] : starts[index + 1]]

    other = to_sibling(normals)
    first = chunk(0)
    first, gamma_slab = together((first, gamma_slab))
    arrived = [from_chips(first)] + [from_chips(chunk(index)) for index in range(1, len(PARTS))]
    gamma_slab, arrived[0] = together((gamma_slab, arrived[0]))

    degrees = freedom_degrees.astype(F32)
    scaling = jnp.sqrt((degrees - 2.0) / degrees / mean_square)[:, None]
    sides = (normals, other, scaling, to_sibling(scaling))
    own_rows, sums = own_moved(*sides, gamma_slab, desk_map, deltas)
    linear = sums[:, :DESKS]

    window_desks = jnp.broadcast_to(desk_map[::STRIDE].astype(F32), (16, per_grp))
    packed = jnp.concatenate([sums[:, DESKS : DESKS + per_grp], window_desks], 0).astype(BF16)
    packed = lax.all_to_all(jnp.broadcast_to(packed, (n_grp,) + packed.shape), "grp", 0, 0, tiled=True)
    desks = packed[:, scenarios].reshape(-1)
    hot = (desks[:, None] == jnp.arange(DESKS).astype(BF16)[None, :]).astype(BF16)
    own_hot, other_hot = window_of(hot, 0)
    window = packed[:, :scenarios].transpose(1, 0, 2).reshape(scenarios, n_grp * per_grp)
    window = jnp.concatenate([window, to_sibling(window)], 0)
    own_window, other_window = window_of(window, 1)

    moved = None
    for index in range(EARLY):
        moved = add_moved(*sides, arrived[index], starts[index], moved)
    mine, theirs = early_terms(linear, own_rows, own_window, own_hot, moved, other_window, other_hot)
    mine = (mine + to_sibling(theirs)).reshape(n_grp, block, DESKS)
    early = lax.all_to_all(mine, "grp", 0, 0, tiled=True).sum(0)

    moved = None
    for index in range(EARLY, last - 1):
        moved = add_moved(*sides, arrived[index], starts[index], moved)
    ready = (arrived[last - 1], early, normals[:, starts[last] :], other[:, starts[last] :])
    next_to_last, early, own_end, other_end = together(ready)
    terms = middle_terms(*sides, next_to_last, starts[last - 1], moved, other_window, other_hot)
    rest = (arrived[last], terms, other_window, other_hot)
    theirs = late_terms(grp, n_grp, 1, BF16, other_end, sides[3], *rest)
    mine = late_terms(grp, n_grp, 0, F32, own_end, sides[2], *rest)
    late = mine + to_sibling(theirs).astype(F32)
    late = late.reshape(n_grp, block, DESKS)
    bit, width = 1, min(4, n_grp)
    while bit < n_grp:
        parts = late.reshape(late.shape[0] // width, width, block, DESKS)
        late = parts[:, 0]
        for step in range(1, width):
            pairs = [(i, i ^ (step * bit)) for i in range(n_grp)]
            late = late + lax.ppermute(parts[:, step].astype(BF16), "grp", pairs).astype(F32)
        bit, width = bit * width, 2
    return early + late[0]


def solution(mesh):
    in_specs = (P("blk", "grp"), P("blk"), P("blk"), P("blk", "grp"), P("grp"), P("grp"))
    out_specs = P(("blk", "grp"), None)
    body = functools.partial(local, mesh.shape["blk"], mesh.shape["grp"])
    return jax.shard_map(body, mesh=mesh, in_specs=in_specs, out_specs=out_specs, check_vma=False)
```

```python
import functools

import jax
import jax.numpy as jnp
from jax import lax
from jax.experimental import pallas as pl
from jax.experimental.pallas import tpu as pltpu
from jax.sharding import PartitionSpec as P

DESKS = 128
STRIDE = 128
CORES = 2
PARTS = (5, 15, 8, 3, 1)
EARLY = 2
VMEM_BYTES = 40 * 2**20

F32 = jnp.float32
BF16 = jnp.bfloat16


def dot_t(left, right):
    return lax.dot_general(left, right, (((1,), (1,)), ((), ())), preferred_element_type=F32)


def call(kernel, **options):
    return pl.pallas_call(
        kernel, compiler_params=pltpu.CompilerParams(vmem_limit_bytes=VMEM_BYTES), **options
    )


def whole(shape):
    return pl.BlockSpec(shape, lambda *_: (0,) * len(shape))


def scaled(normals_ref, scaling_ref):
    return (normals_ref[...].astype(F32) * scaling_ref[...]).astype(BF16)


def own_kernel(own_ref, sibling_ref, own_scaling_ref, sibling_scaling_ref, gamma_ref, desks_ref, deltas_ref, moved_ref, sums_ref):
    step = pl.program_id(0)
    half, width = own_ref.shape

    @pl.when(step == 0)
    def _():
        moved_ref[...] = jnp.zeros_like(moved_ref)
        sums_ref[...] = jnp.zeros_like(sums_ref)

    level = lax.broadcasted_iota(jnp.int32, (DESKS, width), 0)
    factor = lax.broadcasted_iota(jnp.int32, (STRIDE, width), 1) + step * width
    entry = lax.broadcasted_iota(jnp.int32, (STRIDE, width), 0)
    weights = jnp.where(level == desks_ref[...], deltas_ref[...], 0.0).astype(BF16)
    chosen = jnp.where(factor == entry * STRIDE, 1.0, 0.0).astype(BF16)
    own, gamma = scaled(own_ref, own_scaling_ref), gamma_ref[...]
    sums_ref[...] += dot_t(own, jnp.concatenate([weights, chosen], 0))
    moved_ref[:half] += dot_t(own, gamma)
    moved_ref[half:] += dot_t(scaled(sibling_ref, sibling_scaling_ref), gamma)


def own_moved(own, sibling, own_scaling, sibling_scaling, gamma, desks, deltas):
    rows, (count, cols) = own.shape[0], gamma.shape
    width = min(cols, 1024)
    normals = pl.BlockSpec((rows, width), lambda j: (0, j))
    vector = pl.BlockSpec((1, width), lambda j: (0, j))
    return call(
        own_kernel,
        grid=(cols // width,),
        in_specs=[normals, normals, whole((rows, 1)), whole((rows, 1))]
        + [pl.BlockSpec((count, width), lambda j: (0, j)), vector, vector],
        out_specs=[whole((2 * rows, count)), whole((rows, DESKS + STRIDE))],
        out_shape=[
            jax.ShapeDtypeStruct((2 * rows, count), F32),
            jax.ShapeDtypeStruct((rows, DESKS + STRIDE), F32),
        ],
        name="own_rows",
    )(own, sibling, own_scaling, sibling_scaling, gamma, desks[None, :], deltas.astype(F32)[None, :])


def moved_kernel(has_start, *refs):
    own_ref, sibling_ref, own_scaling_ref, sibling_scaling_ref, gamma_ref, *start_ref, out_ref = refs
    half = own_ref.shape[0]

    @pl.when(pl.program_id(0) == 0)
    def _():
        out_ref[...] = start_ref[0][...] if has_start else jnp.zeros_like(out_ref)

    gamma = gamma_ref[...]
    out_ref[:half] += dot_t(scaled(own_ref, own_scaling_ref), gamma)
    out_ref[half:] += dot_t(scaled(sibling_ref, sibling_scaling_ref), gamma)


def add_moved(own, sibling, own_scaling, sibling_scaling, gamma, first, start=None):
    rows, (count, cols) = own.shape[0], gamma.shape
    width = next(size for size in (1024, 512, 256, 128) if cols % size == 0 and first % size == 0)
    normals = pl.BlockSpec((rows, width), lambda j: (0, j + first // width))
    return call(
        functools.partial(moved_kernel, start is not None),
        grid=(cols // width,),
        in_specs=[normals, normals, whole((rows, 1)), whole((rows, 1))]
        + [pl.BlockSpec((count, width), lambda j: (0, j))]
        + [whole((2 * rows, count))] * (start is not None),
        out_specs=whole((2 * rows, count)),
        out_shape=jax.ShapeDtypeStruct((2 * rows, count), F32),
        name="moved",
    )(own, sibling, own_scaling, sibling_scaling, gamma, *([] if start is None else [start]))


def by_desk(moved, window, hot, pieces=3):
    quadratic = 0.5 * window.astype(F32) * moved
    total = None
    for _ in range(pieces):
        piece = quadratic.astype(BF16)
        quadratic = quadratic - piece.astype(F32)
        product = jnp.dot(piece, hot, preferred_element_type=F32)
        total = product if total is None else total + product
    return total


def early_kernel(linear_ref, *refs):
    *groups, mine_ref, theirs_ref = refs
    half = mine_ref.shape[0]
    total = None
    for index in range(0, len(groups), 3):
        moved_ref, window_ref, hot_ref = groups[index : index + 3]
        terms = by_desk(moved_ref[...], window_ref[...], hot_ref[...])
        total = terms if total is None else total + terms
    mine_ref[...] = total[:half] + linear_ref[...]
    theirs_ref[...] = total[half:]


def early_terms(linear, *groups):
    shape = jax.ShapeDtypeStruct(linear.shape, F32)
    return call(early_kernel, out_shape=[shape, shape], name="early")(linear, *groups)


def middle_kernel(own_ref, sibling_ref, own_scaling_ref, sibling_scaling_ref, gamma_ref, start_ref, window_ref, hot_ref, terms_ref, moved_ref):
    step = pl.program_id(0)
    half = own_ref.shape[0]

    @pl.when(step == 0)
    def _():
        moved_ref[...] = start_ref[...]

    gamma = gamma_ref[...]
    moved_ref[:half] += dot_t(scaled(own_ref, own_scaling_ref), gamma)
    moved_ref[half:] += dot_t(scaled(sibling_ref, sibling_scaling_ref), gamma)

    @pl.when(step == pl.num_programs(0) - 1)
    def _():
        terms_ref[...] = by_desk(moved_ref[...], window_ref[...], hot_ref[...], 2)


def middle_terms(own, sibling, own_scaling, sibling_scaling, gamma, first, start, window, hot):
    rows, (count, cols) = own.shape[0], gamma.shape
    width = next(size for size in (512, 256, 128) if cols % size == 0 and first % size == 0)
    normals = pl.BlockSpec((rows, width), lambda j: (0, j + first // width))
    return call(
        middle_kernel,
        grid=(cols // width,),
        in_specs=[normals, normals, whole((rows, 1)), whole((rows, 1))]
        + [pl.BlockSpec((count, width), lambda j: (0, j))]
        + [whole(shape) for shape in (start.shape, window.shape, hot.shape)],
        out_specs=whole((2 * rows, DESKS)),
        out_shape=jax.ShapeDtypeStruct((2 * rows, DESKS), F32),
        scratch_shapes=[pltpu.VMEM((2 * rows, count), F32)],
        name="middle",
    )(own, sibling, own_scaling, sibling_scaling, gamma, start, window, hot)


def late_kernel(blocks, first, grp_ref, normals_ref, scaling_ref, gamma_ref, start_ref, window_ref, hot_ref, out_ref, terms_ref):
    half = normals_ref.shape[0]
    place = slice(first, first + half)
    moved = dot_t(scaled(normals_ref, scaling_ref), gamma_ref[...])
    terms_ref[...] = start_ref[place] + by_desk(moved, window_ref[place], hot_ref[...], 1)
    height = half // blocks
    for index in range(blocks):
        source = pl.multiple_of((index ^ grp_ref[0]) * height, height)
        out_ref[index * height : (index + 1) * height, :] = terms_ref[pl.ds(source, height), :].astype(out_ref.dtype)


def late_terms(grp, blocks, side, kind, normals, scaling, gamma, start, window, hot):
    rows = normals.shape[0]
    in_vmem = pl.BlockSpec(memory_space=pltpu.VMEM)
    return pl.pallas_call(
        functools.partial(late_kernel, blocks, side * rows),
        in_specs=[pl.BlockSpec(memory_space=pltpu.SMEM)] + [in_vmem] * 6,
        out_specs=in_vmem,
        scratch_shapes=[pltpu.VMEM((rows, DESKS), F32)],
        out_shape=jax.ShapeDtypeStruct((rows, DESKS), kind),
        compiler_params=pltpu.CompilerParams(vmem_limit_bytes=12 * 2**20),
        name="late",
    )(grp[None], normals, scaling, gamma, start, window, hot)


def local(n_blk, n_grp, normals, mean_square, freedom_degrees, gamma_slab, deltas, desk_map):
    together = lax.optimization_barrier
    blk, grp = lax.axis_index("blk"), lax.axis_index("grp")
    scenarios, columns = normals.shape
    rows = gamma_slab.shape[0]
    chips = n_blk // CORES
    block = scenarios // n_grp
    per_grp = columns // STRIDE
    sibling = [(i, i ^ 1) for i in range(n_blk)]

    def to_sibling(array):
        return lax.ppermute(array, "blk", sibling)

    def from_chips(array):
        parts = [
            lax.ppermute(array, "blk", [(i, (i + CORES * step) % n_blk) for i in range(n_blk)])
            for step in range(1, chips)
        ]
        return parts[0] if len(parts) == 1 else jnp.concatenate(parts, 0)

    def window_of(array, axis):
        own = lax.dynamic_slice_in_dim(array, blk * rows, rows, axis)
        others = [
            lax.dynamic_slice_in_dim(array, lax.rem(blk + n_blk - CORES * step, n_blk) * rows, rows, axis)
            for step in range(1, chips)
        ]
        return own, others[0] if len(others) == 1 else jnp.concatenate(others, axis)

    unit = columns // sum(PARTS)
    starts = [sum(PARTS[:i]) * unit for i in range(len(PARTS) + 1)]
    last = len(PARTS) - 1

    def chunk(index):
        return gamma_slab[:, starts[index] : starts[index + 1]]

    first = chunk(0)
    first, gamma_slab, normals = together((first, gamma_slab, normals))
    other = to_sibling(normals)
    arrived = [from_chips(first)] + [from_chips(chunk(index)) for index in range(1, len(PARTS))]
    gamma_slab, arrived[0] = together((gamma_slab, arrived[0]))

    degrees = freedom_degrees.astype(F32)
    scaling = jnp.sqrt((degrees - 2.0) / degrees / mean_square)[:, None]
    sides = (normals, other, scaling, to_sibling(scaling))
    own_rows, sums = own_moved(*sides, gamma_slab, desk_map, deltas)
    linear = sums[:, :DESKS]

    window_desks = jnp.broadcast_to(desk_map[::STRIDE].astype(F32), (16, per_grp))
    packed = jnp.concatenate([sums[:, DESKS : DESKS + per_grp], window_desks], 0).astype(BF16)
    packed = lax.all_to_all(jnp.broadcast_to(packed, (n_grp,) + packed.shape), "grp", 0, 0, tiled=True)
    desks = packed[:, scenarios].reshape(-1)
    hot = (desks[:, None] == jnp.arange(DESKS).astype(BF16)[None, :]).astype(BF16)
    own_hot, other_hot = window_of(hot, 0)
    window = packed[:, :scenarios].transpose(1, 0, 2).reshape(scenarios, n_grp * per_grp)
    window = jnp.concatenate([window, to_sibling(window)], 0)
    own_window, other_window = window_of(window, 1)

    moved = None
    for index in range(EARLY):
        moved = add_moved(*sides, arrived[index], starts[index], moved)
    mine, theirs = early_terms(linear, own_rows, own_window, own_hot, moved, other_window, other_hot)
    mine = (mine + to_sibling(theirs)).reshape(n_grp, block, DESKS)
    early = lax.all_to_all(mine, "grp", 0, 0, tiled=True).sum(0)

    moved = None
    for index in range(EARLY, last - 1):
        moved = add_moved(*sides, arrived[index], starts[index], moved)
    ready = (arrived[last - 1], early, normals[:, starts[last] :], other[:, starts[last] :])
    next_to_last, early, own_end, other_end = together(ready)
    terms = middle_terms(*sides, next_to_last, starts[last - 1], moved, other_window, other_hot)
    rest = (arrived[last], terms, other_window, other_hot)
    theirs = late_terms(grp, n_grp, 1, BF16, other_end, sides[3], *rest)
    mine = late_terms(grp, n_grp, 0, F32, own_end, sides[2], *rest)
    late = mine + to_sibling(theirs).astype(F32)
    late = late.reshape(n_grp, block, DESKS)
    bit, width = 1, min(4, n_grp)
    while bit < n_grp:
        parts = late.reshape(late.shape[0] // width, width, block, DESKS)
        late = parts[:, 0]
        for step in range(1, width):
            pairs = [(i, i ^ (step * bit)) for i in range(n_grp)]
            late = late + lax.ppermute(parts[:, step].astype(BF16), "grp", pairs).astype(F32)
        bit, width = bit * width, 2
    return early + late[0]


def solution(mesh):
    in_specs = (P("blk", "grp"), P("blk"), P("blk"), P("blk", "grp"), P("grp"), P("grp"))
    out_specs = P(("blk", "grp"), None)
    body = functools.partial(local, mesh.shape["blk"], mesh.shape["grp"])
    return jax.shard_map(body, mesh=mesh, in_specs=in_specs, out_specs=out_specs, check_vma=False)
```

```python
import functools

import jax
import jax.numpy as jnp
from jax import lax
from jax.experimental import pallas as pl
from jax.experimental.pallas import tpu as pltpu
from jax.sharding import PartitionSpec as P

DESKS = 128
STRIDE = 128
CORES = 2
PARTS = (5, 15, 8, 3, 1)
EARLY = 2
VMEM_BYTES = 40 * 2**20

F32 = jnp.float32
BF16 = jnp.bfloat16


def dot_t(left, right):
    return lax.dot_general(left, right, (((1,), (1,)), ((), ())), preferred_element_type=F32)


def call(kernel, **options):
    return pl.pallas_call(
        kernel, compiler_params=pltpu.CompilerParams(vmem_limit_bytes=VMEM_BYTES), **options
    )


def whole(shape):
    return pl.BlockSpec(shape, lambda *_: (0,) * len(shape))


def scaled(normals_ref, scaling_ref):
    return (normals_ref[...].astype(F32) * scaling_ref[...]).astype(BF16)


def own_kernel(own_ref, sibling_ref, own_scaling_ref, sibling_scaling_ref, gamma_ref, desks_ref, deltas_ref, moved_ref, sums_ref):
    step = pl.program_id(0)
    half, width = own_ref.shape

    @pl.when(step == 0)
    def _():
        moved_ref[...] = jnp.zeros_like(moved_ref)
        sums_ref[...] = jnp.zeros_like(sums_ref)

    level = lax.broadcasted_iota(jnp.int32, (DESKS, width), 0)
    factor = lax.broadcasted_iota(jnp.int32, (STRIDE, width), 1) + step * width
    entry = lax.broadcasted_iota(jnp.int32, (STRIDE, width), 0)
    weights = jnp.where(level == desks_ref[...], deltas_ref[...], 0.0).astype(BF16)
    chosen = jnp.where(factor == entry * STRIDE, 1.0, 0.0).astype(BF16)
    own, gamma = scaled(own_ref, own_scaling_ref), gamma_ref[...]
    sums_ref[...] += dot_t(own, jnp.concatenate([weights, chosen], 0))
    moved_ref[:half] += dot_t(own, gamma)
    moved_ref[half:] += dot_t(scaled(sibling_ref, sibling_scaling_ref), gamma)


def own_moved(own, sibling, own_scaling, sibling_scaling, gamma, desks, deltas):
    rows, (count, cols) = own.shape[0], gamma.shape
    width = min(cols, 1024)
    normals = pl.BlockSpec((rows, width), lambda j: (0, j))
    vector = pl.BlockSpec((1, width), lambda j: (0, j))
    return call(
        own_kernel,
        grid=(cols // width,),
        in_specs=[normals, normals, whole((rows, 1)), whole((rows, 1))]
        + [pl.BlockSpec((count, width), lambda j: (0, j)), vector, vector],
        out_specs=[whole((2 * rows, count)), whole((rows, DESKS + STRIDE))],
        out_shape=[
            jax.ShapeDtypeStruct((2 * rows, count), F32),
            jax.ShapeDtypeStruct((rows, DESKS + STRIDE), F32),
        ],
        name="own_rows",
    )(own, sibling, own_scaling, sibling_scaling, gamma, desks[None, :], deltas.astype(F32)[None, :])


def moved_kernel(has_start, *refs):
    own_ref, sibling_ref, own_scaling_ref, sibling_scaling_ref, gamma_ref, *start_ref, out_ref = refs
    half = own_ref.shape[0]

    @pl.when(pl.program_id(0) == 0)
    def _():
        out_ref[...] = start_ref[0][...] if has_start else jnp.zeros_like(out_ref)

    gamma = gamma_ref[...]
    out_ref[:half] += dot_t(scaled(own_ref, own_scaling_ref), gamma)
    out_ref[half:] += dot_t(scaled(sibling_ref, sibling_scaling_ref), gamma)


def add_moved(own, sibling, own_scaling, sibling_scaling, gamma, first, start=None):
    rows, (count, cols) = own.shape[0], gamma.shape
    width = next(size for size in (1024, 512, 256, 128) if cols % size == 0 and first % size == 0)
    normals = pl.BlockSpec((rows, width), lambda j: (0, j + first // width))
    return call(
        functools.partial(moved_kernel, start is not None),
        grid=(cols // width,),
        in_specs=[normals, normals, whole((rows, 1)), whole((rows, 1))]
        + [pl.BlockSpec((count, width), lambda j: (0, j))]
        + [whole((2 * rows, count))] * (start is not None),
        out_specs=whole((2 * rows, count)),
        out_shape=jax.ShapeDtypeStruct((2 * rows, count), F32),
        name="moved",
    )(own, sibling, own_scaling, sibling_scaling, gamma, *([] if start is None else [start]))


def by_desk(moved, window, hot, pieces=3):
    quadratic = 0.5 * window.astype(F32) * moved
    total = None
    for _ in range(pieces):
        piece = quadratic.astype(BF16)
        quadratic = quadratic - piece.astype(F32)
        product = jnp.dot(piece, hot, preferred_element_type=F32)
        total = product if total is None else total + product
    return total


def early_kernel(linear_ref, *refs):
    *groups, mine_ref, theirs_ref = refs
    half = mine_ref.shape[0]
    total = None
    for index in range(0, len(groups), 3):
        moved_ref, window_ref, hot_ref = groups[index : index + 3]
        terms = by_desk(moved_ref[...], window_ref[...], hot_ref[...])
        total = terms if total is None else total + terms
    mine_ref[...] = total[:half] + linear_ref[...]
    theirs_ref[...] = total[half:]


def early_terms(linear, *groups):
    shape = jax.ShapeDtypeStruct(linear.shape, F32)
    return call(early_kernel, out_shape=[shape, shape], name="early")(linear, *groups)


def middle_kernel(own_ref, sibling_ref, own_scaling_ref, sibling_scaling_ref, gamma_ref, start_ref, window_ref, hot_ref, terms_ref, moved_ref):
    step = pl.program_id(0)
    half = own_ref.shape[0]

    @pl.when(step == 0)
    def _():
        moved_ref[...] = start_ref[...]

    gamma = gamma_ref[...]
    moved_ref[:half] += dot_t(scaled(own_ref, own_scaling_ref), gamma)
    moved_ref[half:] += dot_t(scaled(sibling_ref, sibling_scaling_ref), gamma)

    @pl.when(step == pl.num_programs(0) - 1)
    def _():
        terms_ref[...] = by_desk(moved_ref[...], window_ref[...], hot_ref[...], 2)


def middle_terms(own, sibling, own_scaling, sibling_scaling, gamma, first, start, window, hot):
    rows, (count, cols) = own.shape[0], gamma.shape
    width = next(size for size in (512, 256, 128) if cols % size == 0 and first % size == 0)
    normals = pl.BlockSpec((rows, width), lambda j: (0, j + first // width))
    return call(
        middle_kernel,
        grid=(cols // width,),
        in_specs=[normals, normals, whole((rows, 1)), whole((rows, 1))]
        + [pl.BlockSpec((count, width), lambda j: (0, j))]
        + [whole(shape) for shape in (start.shape, window.shape, hot.shape)],
        out_specs=whole((2 * rows, DESKS)),
        out_shape=jax.ShapeDtypeStruct((2 * rows, DESKS), F32),
        scratch_shapes=[pltpu.VMEM((2 * rows, count), F32)],
        name="middle",
    )(own, sibling, own_scaling, sibling_scaling, gamma, start, window, hot)


def turns(block, width):
    return (int(block % width != 0) + (block // width).bit_count()) % 2 == 1


def late_kernel(
    blocks,
    width,
    for_sibling,
    grp_ref,
    own_ref,
    sibling_ref,
    own_scaling_ref,
    sibling_scaling_ref,
    gamma_ref,
    start_ref,
    window_ref,
    hot_ref,
    out_ref,
    shocks_ref,
    weights_ref,
):
    half = own_ref.shape[0]
    height = half // blocks
    places = []
    for index in range(blocks):
        source = pl.multiple_of((index ^ grp_ref[0]) * height, height)
        here, there = pl.ds(index * height, height), pl.ds(source, height)
        if for_sibling != turns(index, width):
            normals, scaling, both = sibling_ref[there, :], sibling_scaling_ref[there, :], pl.ds(half + source, height)
        else:
            normals, scaling, both = own_ref[there, :], own_scaling_ref[there, :], there
        shocks_ref[here, :] = (normals.astype(F32) * scaling).astype(BF16)
        weights_ref[here, :] = window_ref[both, :]
        places.append((here, both))
    sums = by_desk(dot_t(shocks_ref[...], gamma_ref[...]), weights_ref[...], hot_ref[...], 1)
    for index, (here, both) in enumerate(places):
        block = sums[index * height : (index + 1) * height] + start_ref[both, :]
        out_ref[here, :] = block.astype(out_ref.dtype)


def late_terms(grp, blocks, width, for_sibling, own, sibling, own_scaling, sibling_scaling, gamma, start, window, hot):
    rows, cols = own.shape
    in_vmem = pl.BlockSpec(memory_space=pltpu.VMEM)
    return pl.pallas_call(
        functools.partial(late_kernel, blocks, width, for_sibling),
        in_specs=[pl.BlockSpec(memory_space=pltpu.SMEM)] + [in_vmem] * 8,
        out_specs=in_vmem,
        scratch_shapes=[pltpu.VMEM((rows, cols), BF16), pltpu.VMEM((rows, window.shape[1]), BF16)],
        out_shape=jax.ShapeDtypeStruct((rows, DESKS), BF16 if for_sibling else F32),
        compiler_params=pltpu.CompilerParams(vmem_limit_bytes=12 * 2**20),
        name="late",
    )(grp[None], own, sibling, own_scaling, sibling_scaling, gamma, start, window, hot)


def local(n_blk, n_grp, normals, mean_square, freedom_degrees, gamma_slab, deltas, desk_map):
    together = lax.optimization_barrier
    blk, grp = lax.axis_index("blk"), lax.axis_index("grp")
    scenarios, columns = normals.shape
    rows = gamma_slab.shape[0]
    chips = n_blk // CORES
    block = scenarios // n_grp
    per_grp = columns // STRIDE
    sibling = [(i, i ^ 1) for i in range(n_blk)]

    def to_sibling(array):
        return lax.ppermute(array, "blk", sibling)

    def from_chips(array):
        parts = [
            lax.ppermute(array, "blk", [(i, (i + CORES * step) % n_blk) for i in range(n_blk)])
            for step in range(1, chips)
        ]
        return parts[0] if len(parts) == 1 else jnp.concatenate(parts, 0)

    def window_of(array, axis):
        own = lax.dynamic_slice_in_dim(array, blk * rows, rows, axis)
        others = [
            lax.dynamic_slice_in_dim(array, lax.rem(blk + n_blk - CORES * step, n_blk) * rows, rows, axis)
            for step in range(1, chips)
        ]
        return own, others[0] if len(others) == 1 else jnp.concatenate(others, axis)

    unit = columns // sum(PARTS)
    starts = [sum(PARTS[:i]) * unit for i in range(len(PARTS) + 1)]
    last = len(PARTS) - 1

    def chunk(index):
        return gamma_slab[:, starts[index] : starts[index + 1]]

    first = chunk(0)
    first, gamma_slab, normals = together((first, gamma_slab, normals))
    other = to_sibling(normals)
    arrived = [from_chips(first)] + [from_chips(chunk(index)) for index in range(1, len(PARTS))]
    gamma_slab, arrived[0] = together((gamma_slab, arrived[0]))

    degrees = freedom_degrees.astype(F32)
    scaling = jnp.sqrt((degrees - 2.0) / degrees / mean_square)[:, None]
    sides = (normals, other, scaling, to_sibling(scaling))
    own_rows, sums = own_moved(*sides, gamma_slab, desk_map, deltas)
    linear = sums[:, :DESKS]

    window_desks = jnp.broadcast_to(desk_map[::STRIDE].astype(F32), (16, per_grp))
    packed = jnp.concatenate([sums[:, DESKS : DESKS + per_grp], window_desks], 0).astype(BF16)
    packed = lax.all_to_all(jnp.broadcast_to(packed, (n_grp,) + packed.shape), "grp", 0, 0, tiled=True)
    desks = packed[:, scenarios].reshape(-1)
    hot = (desks[:, None] == jnp.arange(DESKS).astype(BF16)[None, :]).astype(BF16)
    own_hot, other_hot = window_of(hot, 0)
    window = packed[:, :scenarios].transpose(1, 0, 2).reshape(scenarios, n_grp * per_grp)
    window = jnp.concatenate([window, to_sibling(window)], 0)
    own_window, other_window = window_of(window, 1)

    moved = None
    for index in range(EARLY):
        moved = add_moved(*sides, arrived[index], starts[index], moved)
    mine, theirs = early_terms(linear, own_rows, own_window, own_hot, moved, other_window, other_hot)
    mine = (mine + to_sibling(theirs)).reshape(n_grp, block, DESKS)
    early = lax.all_to_all(mine, "grp", 0, 0, tiled=True).sum(0)

    moved = None
    for index in range(EARLY, last - 1):
        moved = add_moved(*sides, arrived[index], starts[index], moved)
    ready = (arrived[last - 1], early, normals[:, starts[last] :], other[:, starts[last] :])
    next_to_last, early, own_end, other_end = together(ready)
    terms = middle_terms(*sides, next_to_last, starts[last - 1], moved, other_window, other_hot)
    width = min(4, n_grp)
    rest = (own_end, other_end, *sides[2:], arrived[last], terms, other_window, other_hot)
    theirs = late_terms(grp, n_grp, width, True, *rest)
    mine = late_terms(grp, n_grp, width, False, *rest)
    late = mine + to_sibling(theirs).astype(F32)
    late = late.reshape(n_grp, block, DESKS)
    bit = 1
    while bit < n_grp:
        parts = late.reshape(late.shape[0] // width, width, block, DESKS)
        late = parts[:, 0]
        for step in range(1, width):
            pairs = [
                (i * n_grp + j, (i ^ 1) * n_grp + (j ^ (step * bit))) for i in range(n_blk) for j in range(n_grp)
            ]
            late = late + lax.ppermute(parts[:, step].astype(BF16), ("blk", "grp"), pairs).astype(F32)
        bit, width = bit * width, 2
    return early + late[0]


def solution(mesh):
    in_specs = (P("blk", "grp"), P("blk"), P("blk"), P("blk", "grp"), P("grp"), P("grp"))
    out_specs = P(("blk", "grp"), None)
    body = functools.partial(local, mesh.shape["blk"], mesh.shape["grp"])
    return jax.shard_map(body, mesh=mesh, in_specs=in_specs, out_specs=out_specs, check_vma=False)
```

```python
import functools

import jax
import jax.numpy as jnp
from jax import lax
from jax.experimental import pallas as pl
from jax.experimental.pallas import tpu as pltpu
from jax.sharding import PartitionSpec as P

DESKS = 128
STRIDE = 128
CORES = 2
PARTS = (5, 15, 8, 3, 1)
EARLY = 2
VMEM_BYTES = 40 * 2**20

F32 = jnp.float32
BF16 = jnp.bfloat16


def dot_t(left, right):
    return lax.dot_general(left, right, (((1,), (1,)), ((), ())), preferred_element_type=F32)


def call(kernel, **options):
    return pl.pallas_call(
        kernel, compiler_params=pltpu.CompilerParams(vmem_limit_bytes=VMEM_BYTES), **options
    )


def whole(shape):
    return pl.BlockSpec(shape, lambda *_: (0,) * len(shape))


def scaled(normals_ref, scaling_ref):
    return (normals_ref[...].astype(F32) * scaling_ref[...]).astype(BF16)


def own_kernel(own_ref, sibling_ref, own_scaling_ref, sibling_scaling_ref, gamma_ref, desks_ref, deltas_ref, moved_ref, sums_ref):
    step = pl.program_id(0)
    half, width = own_ref.shape

    @pl.when(step == 0)
    def _():
        moved_ref[...] = jnp.zeros_like(moved_ref)
        sums_ref[...] = jnp.zeros_like(sums_ref)

    level = lax.broadcasted_iota(jnp.int32, (DESKS, width), 0)
    factor = lax.broadcasted_iota(jnp.int32, (STRIDE, width), 1) + step * width
    entry = lax.broadcasted_iota(jnp.int32, (STRIDE, width), 0)
    weights = jnp.where(level == desks_ref[...], deltas_ref[...], 0.0).astype(BF16)
    chosen = jnp.where(factor == entry * STRIDE, 1.0, 0.0).astype(BF16)
    own, gamma = scaled(own_ref, own_scaling_ref), gamma_ref[...]
    sums_ref[...] += dot_t(own, jnp.concatenate([weights, chosen], 0))
    moved_ref[:half] += dot_t(own, gamma)
    moved_ref[half:] += dot_t(scaled(sibling_ref, sibling_scaling_ref), gamma)


def own_moved(own, sibling, own_scaling, sibling_scaling, gamma, desks, deltas):
    rows, (count, cols) = own.shape[0], gamma.shape
    width = min(cols, 1024)
    normals = pl.BlockSpec((rows, width), lambda j: (0, j))
    vector = pl.BlockSpec((1, width), lambda j: (0, j))
    return call(
        own_kernel,
        grid=(cols // width,),
        in_specs=[normals, normals, whole((rows, 1)), whole((rows, 1))]
        + [pl.BlockSpec((count, width), lambda j: (0, j)), vector, vector],
        out_specs=[whole((2 * rows, count)), whole((rows, DESKS + STRIDE))],
        out_shape=[
            jax.ShapeDtypeStruct((2 * rows, count), F32),
            jax.ShapeDtypeStruct((rows, DESKS + STRIDE), F32),
        ],
        name="own_rows",
    )(own, sibling, own_scaling, sibling_scaling, gamma, desks[None, :], deltas.astype(F32)[None, :])


def moved_kernel(has_start, *refs):
    own_ref, sibling_ref, own_scaling_ref, sibling_scaling_ref, gamma_ref, *start_ref, out_ref = refs
    half = own_ref.shape[0]

    @pl.when(pl.program_id(0) == 0)
    def _():
        out_ref[...] = start_ref[0][...] if has_start else jnp.zeros_like(out_ref)

    gamma = gamma_ref[...]
    out_ref[:half] += dot_t(scaled(own_ref, own_scaling_ref), gamma)
    out_ref[half:] += dot_t(scaled(sibling_ref, sibling_scaling_ref), gamma)


def add_moved(own, sibling, own_scaling, sibling_scaling, gamma, first, start=None):
    rows, (count, cols) = own.shape[0], gamma.shape
    width = next(size for size in (1024, 512, 256, 128) if cols % size == 0 and first % size == 0)
    normals = pl.BlockSpec((rows, width), lambda j: (0, j + first // width))
    return call(
        functools.partial(moved_kernel, start is not None),
        grid=(cols // width,),
        in_specs=[normals, normals, whole((rows, 1)), whole((rows, 1))]
        + [pl.BlockSpec((count, width), lambda j: (0, j))]
        + [whole((2 * rows, count))] * (start is not None),
        out_specs=whole((2 * rows, count)),
        out_shape=jax.ShapeDtypeStruct((2 * rows, count), F32),
        name="moved",
    )(own, sibling, own_scaling, sibling_scaling, gamma, *([] if start is None else [start]))


def by_desk(moved, window, hot, pieces=3):
    quadratic = 0.5 * window.astype(F32) * moved
    total = None
    for _ in range(pieces):
        piece = quadratic.astype(BF16)
        quadratic = quadratic - piece.astype(F32)
        product = jnp.dot(piece, hot, preferred_element_type=F32)
        total = product if total is None else total + product
    return total


def early_kernel(linear_ref, *refs):
    *groups, mine_ref, theirs_ref = refs
    half = mine_ref.shape[0]
    total = None
    for index in range(0, len(groups), 3):
        moved_ref, window_ref, hot_ref = groups[index : index + 3]
        terms = by_desk(moved_ref[...], window_ref[...], hot_ref[...])
        total = terms if total is None else total + terms
    mine_ref[...] = total[:half] + linear_ref[...]
    theirs_ref[...] = total[half:]


def early_terms(linear, *groups):
    shape = jax.ShapeDtypeStruct(linear.shape, F32)
    return call(early_kernel, out_shape=[shape, shape], name="early")(linear, *groups)


def middle_kernel(own_ref, sibling_ref, own_scaling_ref, sibling_scaling_ref, gamma_ref, start_ref, window_ref, hot_ref, terms_ref, moved_ref):
    step = pl.program_id(0)
    half = own_ref.shape[0]

    @pl.when(step == 0)
    def _():
        moved_ref[...] = start_ref[...]

    gamma = gamma_ref[...]
    moved_ref[:half] += dot_t(scaled(own_ref, own_scaling_ref), gamma)
    moved_ref[half:] += dot_t(scaled(sibling_ref, sibling_scaling_ref), gamma)

    @pl.when(step == pl.num_programs(0) - 1)
    def _():
        terms_ref[...] = by_desk(moved_ref[...], window_ref[...], hot_ref[...], 2)


def middle_terms(own, sibling, own_scaling, sibling_scaling, gamma, first, start, window, hot):
    rows, (count, cols) = own.shape[0], gamma.shape
    width = next(size for size in (512, 256, 128) if cols % size == 0 and first % size == 0)
    normals = pl.BlockSpec((rows, width), lambda j: (0, j + first // width))
    return call(
        middle_kernel,
        grid=(cols // width,),
        in_specs=[normals, normals, whole((rows, 1)), whole((rows, 1))]
        + [pl.BlockSpec((count, width), lambda j: (0, j))]
        + [whole(shape) for shape in (start.shape, window.shape, hot.shape)],
        out_specs=whole((2 * rows, DESKS)),
        out_shape=jax.ShapeDtypeStruct((2 * rows, DESKS), F32),
        scratch_shapes=[pltpu.VMEM((2 * rows, count), F32)],
        name="middle",
    )(own, sibling, own_scaling, sibling_scaling, gamma, start, window, hot)


def turns(block, width):
    return (int(block % width != 0) + (block // width).bit_count()) % 2 == 1


def late_kernel(
    blocks,
    width,
    for_sibling,
    grp_ref,
    own_ref,
    sibling_ref,
    own_scaling_ref,
    sibling_scaling_ref,
    gamma_ref,
    start_ref,
    window_ref,
    hot_ref,
    out_ref,
    shocks_ref,
    weights_ref,
):
    half = own_ref.shape[0]
    height = half // blocks
    places = []
    for index in range(blocks):
        source = pl.multiple_of((index ^ grp_ref[0]) * height, height)
        here, there = pl.ds(index * height, height), pl.ds(source, height)
        if for_sibling != turns(index, width):
            normals, scaling, both = sibling_ref[there, :], sibling_scaling_ref[there, :], pl.ds(half + source, height)
        else:
            normals, scaling, both = own_ref[there, :], own_scaling_ref[there, :], there
        shocks_ref[here, :] = (normals.astype(F32) * scaling).astype(BF16)
        weights_ref[here, :] = window_ref[both, :]
        places.append((here, both))
    sums = by_desk(dot_t(shocks_ref[...], gamma_ref[...]), weights_ref[...], hot_ref[...], 1)
    for index, (here, both) in enumerate(places):
        block = sums[index * height : (index + 1) * height] + start_ref[both, :]
        out_ref[here, :] = block.astype(out_ref.dtype)


def late_terms(grp, blocks, width, for_sibling, own, sibling, own_scaling, sibling_scaling, gamma, start, window, hot):
    rows, cols = own.shape
    in_vmem = pl.BlockSpec(memory_space=pltpu.VMEM)
    return pl.pallas_call(
        functools.partial(late_kernel, blocks, width, for_sibling),
        in_specs=[pl.BlockSpec(memory_space=pltpu.SMEM)] + [in_vmem] * 8,
        out_specs=in_vmem,
        scratch_shapes=[pltpu.VMEM((rows, cols), BF16), pltpu.VMEM((rows, window.shape[1]), BF16)],
        out_shape=jax.ShapeDtypeStruct((rows, DESKS), BF16 if for_sibling else F32),
        compiler_params=pltpu.CompilerParams(vmem_limit_bytes=12 * 2**20),
        name="late",
    )(grp[None], own, sibling, own_scaling, sibling_scaling, gamma, start, window, hot)


def local(n_blk, n_grp, normals, mean_square, freedom_degrees, gamma_slab, deltas, desk_map):
    together = lax.optimization_barrier
    blk, grp = lax.axis_index("blk"), lax.axis_index("grp")
    scenarios, columns = normals.shape
    rows = gamma_slab.shape[0]
    chips = n_blk // CORES
    block = scenarios // n_grp
    per_grp = columns // STRIDE
    sibling = [(i, i ^ 1) for i in range(n_blk)]

    def to_sibling(array):
        return lax.ppermute(array, "blk", sibling)

    def from_chips(array):
        parts = [
            lax.ppermute(array, "blk", [(i, (i + CORES * step) % n_blk) for i in range(n_blk)])
            for step in range(1, chips)
        ]
        return parts[0] if len(parts) == 1 else jnp.concatenate(parts, 0)

    def window_of(array, axis):
        own = lax.dynamic_slice_in_dim(array, blk * rows, rows, axis)
        others = [
            lax.dynamic_slice_in_dim(array, lax.rem(blk + n_blk - CORES * step, n_blk) * rows, rows, axis)
            for step in range(1, chips)
        ]
        return own, others[0] if len(others) == 1 else jnp.concatenate(others, axis)

    unit = columns // sum(PARTS)
    starts = [sum(PARTS[:i]) * unit for i in range(len(PARTS) + 1)]
    last = len(PARTS) - 1

    def chunk(index):
        return gamma_slab[:, starts[index] : starts[index + 1]]

    first = chunk(0)
    first, gamma_slab, normals = together((first, gamma_slab, normals))
    other = to_sibling(normals)
    arrived = [from_chips(first)] + [from_chips(chunk(index)) for index in range(1, len(PARTS))]
    gamma_slab, arrived[0] = together((gamma_slab, arrived[0]))

    degrees = freedom_degrees.astype(F32)
    scaling = jnp.sqrt((degrees - 2.0) / degrees / mean_square)[:, None]
    sides = (normals, other, scaling, to_sibling(scaling))
    own_rows, sums = own_moved(*sides, gamma_slab, desk_map, deltas)
    linear = sums[:, :DESKS]

    window_desks = jnp.broadcast_to(desk_map[::STRIDE].astype(F32), (16, per_grp))
    packed = jnp.concatenate([sums[:, DESKS : DESKS + per_grp], window_desks], 0).astype(BF16)
    packed = lax.all_to_all(jnp.broadcast_to(packed, (n_grp,) + packed.shape), "grp", 0, 0, tiled=True)
    desks = packed[:, scenarios].reshape(-1)
    hot = (desks[:, None] == jnp.arange(DESKS).astype(BF16)[None, :]).astype(BF16)
    own_hot, other_hot = window_of(hot, 0)
    window = packed[:, :scenarios].transpose(1, 0, 2).reshape(scenarios, n_grp * per_grp)
    window = jnp.concatenate([window, to_sibling(window)], 0)
    own_window, other_window = window_of(window, 1)

    moved = None
    for index in range(EARLY):
        moved = add_moved(*sides, arrived[index], starts[index], moved)
    mine, theirs = early_terms(linear, own_rows, own_window, own_hot, moved, other_window, other_hot)
    mine = (mine + to_sibling(theirs)).reshape(n_grp, block, DESKS)
    early = lax.all_to_all(mine, "grp", 0, 0, tiled=True).sum(0)

    moved = None
    for index in range(EARLY, last - 1):
        moved = add_moved(*sides, arrived[index], starts[index], moved)
    ready = (arrived[last - 1], early, normals[:, starts[last] :], other[:, starts[last] :])
    next_to_last, early, own_end, other_end = together(ready)
    terms = middle_terms(*sides, next_to_last, starts[last - 1], moved, other_window, other_hot)
    width = min(4, n_grp)
    rest = (own_end, other_end, *sides[2:], arrived[last], terms, other_window, other_hot)
    theirs = late_terms(grp, n_grp, width, True, *rest)
    mine = late_terms(grp, n_grp, width, False, *rest)
    late = mine + to_sibling(theirs).astype(F32)
    late = late.reshape(n_grp, block, DESKS)
    bit = 1
    while bit < n_grp:
        parts = late.reshape(late.shape[0] // width, width, block, DESKS)
        late = parts[:, 0]
        for step in range(width - 1, 0, -1):
            pairs = [
                (i * n_grp + j, (i ^ 1) * n_grp + (j ^ (step * bit))) for i in range(n_blk) for j in range(n_grp)
            ]
            late = late + lax.ppermute(parts[:, step].astype(BF16), ("blk", "grp"), pairs).astype(F32)
        bit, width = bit * width, 2
    return early + late[0]


def solution(mesh):
    in_specs = (P("blk", "grp"), P("blk"), P("blk"), P("blk", "grp"), P("grp"), P("grp"))
    out_specs = P(("blk", "grp"), None)
    body = functools.partial(local, mesh.shape["blk"], mesh.shape["grp"])
    return jax.shard_map(body, mesh=mesh, in_specs=in_specs, out_specs=out_specs, check_vma=False)
```
